512 devices in a mesh: dp: 4 (over y), expert: 128 (over x, z, core).
Axes of the slice: x: 4, y: 4, z: 16, core: 2. Of those that a mesh axis runs over, the one named last changes fastest.
Arguments:
- down_cotangent: bfloat16 [65536, 2560], P(('dp', 'expert')), may hold values from -24 to 24
- saved_hidden: bfloat16 [65536, 6, 768], P(('dp', 'expert')), may hold values from -0.3125 to 0.3125
- route_ids: int32 [65536, 6], P(('dp', 'expert')), may hold values from 0 to 127, all different within a row; in each aligned block of 128 rows (0 to 127, 128 to 255, ...) at most 10 rows name the same one
- route_gates: bfloat16 [65536, 6], P(('dp', 'expert')), may hold values from 0.049804688 to 0.59765625
- down_weight: bfloat16 [128, 2560, 768], P('expert', 'dp'), may hold values from -0.21875 to 0.21875
Outputs:
- hidden_grad: bfloat16 [65536, 6, 768], P(('dp', 'expert'))
- gate_grad: bfloat16 [65536, 6], P(('dp', 'expert'))
- weight_grad: bfloat16 [128, 2560, 768], P('expert', 'dp')
The draws below stay inside these ranges and needn't reach their ends.
Inputs may be any that keep to these rules, and one draw needn't show every extreme that they name: `route_ids`: each row names 6 different experts. Within the rows of one device (aligned blocks of 128 rows) no expert is named more than 10 times, and in some block one expert is named exactly 10 times.
All inputs are finite; a program needn't handle non-finite values.
Results may differ from the reference program's by a relative error of at most 0.013.
Values may be sent and summed in bfloat16 or wider, within the bound.
No kernel may reach another device: no remote copies, remote signals or barrier semaphores. Data moves between devices by JAX's collectives and lax.ppermute only.
A program may use at most 128 MiB of HBM per device.

```python
import math
import jax
import jax.numpy as jnp
import numpy as np
from jax import lax

D = 2560
F = 768
TOP = 6
TOK_DEV = 128
EXPERTS = 128
SLOT = 10
TOKENS = 65536
N_DP = 4
N_EXPERT = 128


def spiked(drawn, own_key, source, target, blocks, factor):
    owner, partner = [(jnp.arange(drawn.shape[position]) // (drawn.shape[position] // blocks)).reshape([-1 if axis == position else 1 for axis in range(drawn.ndim)]) for position in (source, target)]
    chosen = jax.random.permutation(own_key, blocks)[partner]
    strong = (owner == chosen) | (owner == (partner + blocks // 2) % blocks)
    return jnp.where(strong, factor * drawn, drawn)


def level_of(rng, shape, shards, low, largest):
    def one(position, shards_of):
        heights = jax.random.uniform(jax.random.fold_in(jax.random.fold_in(rng, 6), position), (shards_of,), jnp.float32, low / len(shards), largest / len(shards))
        return jnp.repeat(jnp.exp(heights), shape[position] // shards_of).reshape((-1,) + (1,) * (len(shape) - position - 1))

    gain = one(*shards[0])
    for cut in shards[1:]:
        gain = gain * one(*cut)
    return gain


def shared_out(stream_key, own, number, rows, amount, top, bound, slope):
    sequence = jax.random.permutation(stream_key, amount)
    heavy_load, usual = portions_of(amount, rows * top, bound, slope, True), portions_of(amount, rows * top, bound, slope, False)
    places = jnp.arange(amount)

    def named(sizes, offset_by):
        used = int((sizes > 0).sum())
        fixed = max(1, used // 4)
        shifted = fixed + (places - fixed + offset_by * (used - fixed)) % max(1, amount - fixed)
        return jnp.zeros((amount,), jnp.int32).at[sequence[jnp.where(places < fixed, places, shifted)]].set(jnp.asarray(sizes, jnp.int32))

    sizes = jnp.where(number % 4 == 0, named(heavy_load, number // 4), named(usual, number - number // 4 - 1))
    mixed = jax.random.permutation(jax.random.fold_in(own, 3), amount)
    giver, receiver = mixed[0:amount // 2 * 2:2], mixed[1:amount // 2 * 2:2]
    slack = jnp.minimum(sizes[giver] - 1, bound - sizes[receiver]) // 2
    slack = jnp.where((giver == sequence[0]) | (receiver == sequence[0]) | (sizes[receiver] == 0), 0, jnp.maximum(slack, 0))
    shifted = jax.random.randint(jax.random.fold_in(own, 4), (amount // 2,), 0, 1 << 20) % (slack + 1)
    sizes = sizes.at[giver].add(-shifted).at[receiver].add(shifted)
    members = jnp.searchsorted(jnp.cumsum(sizes), jnp.arange(rows * top), side="right").astype(jnp.int32)
    table = members.reshape(top, rows).T
    table = table[jax.random.permutation(jax.random.fold_in(own, 1), rows)]
    offset_by = jax.random.randint(jax.random.fold_in(own, 2), (rows, 1), 0, top)
    return jnp.take_along_axis(table, (jnp.arange(top)[None, :] + offset_by) % top, axis=1)


def portions_of(amount, total, reach, lean, full):
    weights = [(1 << 20) // math.isqrt(standing ** lean) + 1 for standing in range(1, amount + 1)]
    largest = reach if full else min(reach, max(-(-total // amount), total * weights[0] // sum(weights)))
    least = 1 if total - largest >= amount - 1 else 0
    counts, surplus = [largest] + [least] * (amount - 1), total - largest - least * (amount - 1)
    while surplus > 0:
        free = [i for i in range(1, amount) if counts[i] < largest] or [i for i in range(1, amount) if counts[i] < reach]
        pool, remaining = sum([weights[i] for i in free]), surplus
        for i in free:
            addition = min(reach - counts[i], max(1, remaining * weights[i] // pool), surplus)
            counts[i] = counts[i] + addition
            surplus = surplus - addition
    return np.array(counts)


def scatter_about(own_key, dims, width, reach, pieces=(), kind=jnp.bfloat16):
    result = jax.random.normal(own_key, dims, jnp.float32) * width
    if len(pieces) > 0:
        result = level_of(own_key, dims, pieces, -0.22, 0.18) * result
    return jnp.clip(result, min=-reach, max=reach).astype(kind)


def bell_draw_with(stream_key, extent, deviation, bound, pieces, heavy, held_as=jnp.bfloat16):
    result = deviation * jax.random.normal(stream_key, extent, jnp.float32)
    if pieces:
        result = result * level_of(stream_key, extent, pieces, -0.22, 0.18)
    return jnp.clip(spiked(result, jax.random.fold_in(stream_key, 3), *heavy), -bound, bound).astype(held_as)


def setup_inputs(seed: int = 0) -> dict:
    arg_keys = jax.random.split(jax.random.key(seed), 6)
    down_cotangent = bell_draw_with(arg_keys[0], (TOKENS, D), 1.0, 24.0, ((0, 512),), (0, 1, 512, 6.0))
    saved_hidden = scatter_about(arg_keys[1], (TOKENS, TOP, F), 0.05, 0.3125, ((0, 512),))
    route_ids_keys = jax.random.split(jax.random.fold_in(arg_keys[2], 1), TOKENS // TOK_DEV)
    route_ids_turns = jax.random.permutation(jax.random.fold_in(arg_keys[2], 3), TOKENS // TOK_DEV)
    route_ids = jax.vmap(lambda own, number: shared_out(jax.random.fold_in(arg_keys[2], 2), own, number, TOK_DEV, EXPERTS, TOP, SLOT, 2))(route_ids_keys, route_ids_turns).reshape((TOKENS, TOP))
    route_gates = jnp.clip(0.049804688 + 0.54785156 * jax.random.uniform(arg_keys[3], (TOKENS, TOP), jnp.float32) ** level_of(arg_keys[3], (TOKENS, TOP), ((0, 512),), -0.2, 0.2), 0.049804688, 0.59765625).astype(jnp.bfloat16)
    down_weight = scatter_about(arg_keys[4], (EXPERTS, D, F), F ** -0.5, 0.21875, ((0, 128), (1, 4)))
    return dict(down_cotangent=down_cotangent, saved_hidden=saved_hidden, route_ids=route_ids, route_gates=route_gates, down_weight=down_weight)


def reference(down_cotangent, saved_hidden, route_ids, route_gates, down_weight):
    token_count, top_count = route_ids.shape
    model_width = down_cotangent.shape[1]
    hidden = saved_hidden.shape[2]
    expert_count = down_weight.shape[0]
    pair_count = token_count * top_count
    replica_rows = token_count // N_DP
    group_rows = SLOT * N_EXPERT
    flat_ids = route_ids.reshape(pair_count).astype(jnp.int32)
    pair_index = jnp.arange(pair_count, dtype=jnp.int32)
    replica_of = (pair_index // top_count) // replica_rows
    sort_keys = replica_of * expert_count + flat_ids
    pair_order = jnp.argsort(sort_keys, stable=True).astype(jnp.int32)
    sorted_keys = sort_keys[pair_order]
    group_ids = jnp.arange(N_DP * expert_count, dtype=jnp.int32)
    starts = jnp.searchsorted(sorted_keys, group_ids, side="left").astype(jnp.int32)
    ends_at = jnp.searchsorted(sorted_keys, group_ids, side="right").astype(jnp.int32)
    flat_hidden = saved_hidden.reshape(pair_count, hidden)
    flat_gates = route_gates.reshape(pair_count).astype(jnp.float32)
    within = jnp.arange(group_rows, dtype=jnp.int32)

    def one_expert(carried, expert):
        hidden_grad, gate_grad = carried
        weight = down_weight[expert]
        summed = jnp.zeros((model_width, hidden), jnp.float32)
        for replica in range(N_DP):
            group_index = replica * expert_count + expert
            first_pair = starts[group_index]
            valid_rows = within < ends_at[group_index] - first_pair
            pair_rows = pair_order[jnp.minimum(first_pair + within, pair_count - 1)]
            cot_rows = down_cotangent[pair_rows // top_count]
            hid_rows = flat_hidden[pair_rows]
            gate_rows = jnp.where(valid_rows, flat_gates[pair_rows], 0.0)
            grad_rows = jnp.dot(cot_rows, weight, preferred_element_type=jnp.float32)
            target_rows = jnp.where(valid_rows, pair_rows, pair_count)
            hidden_grad = hidden_grad.at[target_rows].set((gate_rows[:, None] * grad_rows).astype(jnp.bfloat16), mode="drop")
            gate_values = jnp.sum(grad_rows * hid_rows.astype(jnp.float32), axis=1).astype(jnp.bfloat16)
            gate_grad = gate_grad.at[target_rows].set(gate_values, mode="drop")
            scaled = (gate_rows[:, None] * hid_rows.astype(jnp.float32)).astype(jnp.bfloat16)
            replica_part = jnp.dot(cot_rows.T, scaled, preferred_element_type=jnp.float32).astype(jnp.bfloat16)
            replica_part = lax.optimization_barrier(replica_part)
            summed = summed + replica_part.astype(jnp.float32)
        return (hidden_grad, gate_grad), summed.astype(jnp.bfloat16)

    initial = (jnp.zeros((pair_count, hidden), jnp.bfloat16), jnp.zeros((pair_count,), jnp.bfloat16))
    finals, weight_grad = lax.scan(one_expert, initial, jnp.arange(expert_count, dtype=jnp.int32))
    hidden_grad, gate_grad = finals
    return hidden_grad.reshape(token_count, top_count, hidden), gate_grad.reshape(token_count, top_count), weight_grad
```

```python
import jax
import jax.numpy as jnp
from jax import lax
from jax.sharding import PartitionSpec as P

SLOTS = 10


def grid_of(dims):
    nx, nz, nc = dims
    along_z = [
        [(x * nz + z) * nc + c for z in range(nz)] for x in range(nx) for c in range(nc)
    ]
    in_plane = [
        [(x * nz + z) * nc + c for x in range(nx) for c in range(nc)] for z in range(nz)
    ]
    return along_z, in_plane


def on_device(dims, down_cotangent, saved_hidden, route_ids, route_gates, down_weight):
    nx, nz, nc = dims
    along_z, in_plane = grid_of(dims)
    experts, plane = nx * nz * nc, nx * nc
    tokens, top = route_ids.shape
    width, hidden = down_cotangent.shape[1], saved_hidden.shape[2]
    pairs, rows = tokens * top, experts * SLOTS
    lanes = SLOTS * hidden // 128

    ids = route_ids.T
    gates = route_gates.T.reshape(pairs, 1).astype(jnp.float32)
    hid = saved_hidden.transpose(1, 0, 2).reshape(pairs, hidden).astype(jnp.float32)

    named = ids[:, None, :] == jnp.arange(experts, dtype=jnp.int32)[None, :, None]
    member = jnp.any(named, axis=0)
    earlier = jnp.arange(tokens)[:, None] < jnp.arange(tokens)[None, :]
    rank = jnp.dot(
        member.astype(jnp.bfloat16),
        earlier.astype(jnp.bfloat16),
        preferred_element_type=jnp.float32,
    ).astype(jnp.int32)
    within = jnp.sum(jnp.where(named, rank[None], 0), axis=1)
    target = (ids * SLOTS + within).reshape(pairs)

    slot = jnp.arange(SLOTS, dtype=jnp.int32)
    table = jnp.max(
        jnp.where(
            member[:, None, :] & (rank[:, None, :] == slot[None, :, None]),
            jnp.arange(tokens, dtype=jnp.int32)[None, None, :],
            -1,
        ),
        axis=2,
    )
    table = table.reshape(nx, nz, nc * SLOTS).transpose(1, 0, 2).reshape(nz, 1, plane * SLOTS)

    table = lax.all_to_all(
        table, "expert", 0, 0, axis_index_groups=along_z, tiled=True
    ).reshape(nz, plane, SLOTS)

    replicas, replica = lax.axis_size("dp"), lax.axis_index("dp")
    own = down_weight[0]
    weight = jnp.zeros((replicas,) + own.shape, own.dtype)
    for step in range(replicas):
        block = own
        if step:
            block = lax.ppermute(
                own, "dp", [(i, (i - step) % replicas) for i in range(replicas)]
            )
        weight = lax.dynamic_update_index_in_dim(
            weight, block, (replica + step) % replicas, 0
        )
    weight = weight.reshape(width, hidden)

    scaled = (gates * hid).astype(jnp.bfloat16)
    send = (jnp.arange(rows, dtype=jnp.int32)[:, None] == target[None, :]).astype(jnp.bfloat16)
    sent = jnp.dot(send, scaled, preferred_element_type=jnp.float32).astype(jnp.bfloat16)
    sent = sent.reshape(experts, lanes, 128)

    line = lax.all_gather(
        down_cotangent, "expert", axis_index_groups=along_z, axis=0, tiled=True
    )
    line, sent, table, weight = lax.optimization_barrier((line, sent, table, weight))

    half = nz // 2
    line = line.reshape(2, half * tokens, width)
    place = lax.axis_index("expert")
    my_x, my_c = place // (nz * nc), place % nc
    offset = (jnp.arange(nz, dtype=jnp.int32) % half * tokens)[:, None, None]
    pick = jnp.where(table >= 0, table + offset, -1)
    pick = pick.reshape(2, half, nx, nc, SLOTS).transpose(2, 3, 0, 1, 4)
    pick = jnp.roll(jnp.roll(pick, -my_x, axis=0), -my_c, axis=1)
    pick = pick.reshape(plane, 2, half * SLOTS)
    choose = (
        pick[..., None] == jnp.arange(half * tokens, dtype=jnp.int32)[None, None, None, :]
    ).astype(jnp.bfloat16)
    chosen = jnp.einsum("dbrt,btw->dbrw", choose, line, preferred_element_type=jnp.float32)
    chosen = chosen.astype(jnp.bfloat16).reshape(plane, nz * SLOTS, width)
    work_cot, sources = [], []
    for dx in range(nx):
        for dc in range(nc):
            block = chosen[dx * nc + dc]
            if dx or dc:
                moves = [
                    ((x * nz + z) * nc + c, ((x + dx) % nx * nz + z) * nc + (c + dc) % nc)
                    for x in range(nx)
                    for z in range(nz)
                    for c in range(nc)
                ]
                block = lax.ppermute(block, "expert", moves)
            work_cot.append(block)
            sources.append((my_x - dx) % nx * nc + (my_c - dc) % nc)

    got = lax.all_to_all(sent, "expert", 0, 0, tiled=True)
    got = got.reshape(nx, nz, nc, lanes, 128).transpose(0, 2, 1, 3, 4)
    got = got.reshape(plane, nz * SLOTS, hidden)
    work_hid = jnp.concatenate(
        [lax.dynamic_index_in_dim(got, source, 0, keepdims=False) for source in sources]
    )

    back = jnp.zeros((plane, nz * SLOTS, hidden), jnp.bfloat16)
    for part, source in zip(work_cot, sources):
        grad_rows = jnp.dot(part, weight, preferred_element_type=jnp.float32)
        back = lax.dynamic_update_index_in_dim(back, grad_rows.astype(jnp.bfloat16), source, 0)
    back = back.reshape(nx, nc, nz, lanes, 128)
    back = back.transpose(0, 2, 1, 3, 4).reshape(experts, lanes, 128)
    home = lax.all_to_all(back, "expert", 0, 0, tiled=True).reshape(rows, hidden)

    total = lax.dot_general(
        jnp.concatenate(work_cot),
        work_hid,
        (((0,), (0,)), ((), ())),
        preferred_element_type=jnp.float32,
    ).astype(jnp.bfloat16)
    weight_grad = lax.psum_scatter(total, "dp", scatter_dimension=0, tiled=True)

    take = (target[:, None] == jnp.arange(rows, dtype=jnp.int32)[None, :]).astype(jnp.bfloat16)
    mine = jnp.dot(take, home, preferred_element_type=jnp.float32)
    hidden_grad = (gates * mine).astype(jnp.bfloat16)
    gate_grad = jnp.sum(mine * hid, axis=1).astype(jnp.bfloat16)
    hidden_grad = hidden_grad.reshape(top, tokens, hidden).transpose(1, 0, 2)
    return hidden_grad, gate_grad.reshape(top, tokens).T, weight_grad[None]


def solution(mesh):
    dims = (4, 16, 2)
    in_specs = (
        P(("dp", "expert"), None),
        P(("dp", "expert"), None, None),
        P(("dp", "expert"), None),
        P(("dp", "expert"), None),
        P("expert", "dp", None),
    )
    out_specs = (
        P(("dp", "expert"), None, None),
        P(("dp", "expert"), None),
        P("expert", "dp", None),
    )

    def step(*arrays):
        return on_device(dims, *arrays)

    return jax.shard_map(
        step, mesh=mesh, in_specs=in_specs, out_specs=out_specs, check_vma=False
    )
```

```python
import jax
import jax.numpy as jnp
import numpy as np
from jax import lax
from jax.experimental import pallas as pl
from jax.experimental.pallas import tpu as pltpu
from jax.sharding import PartitionSpec as P

SLOTS = 10


def grid_of(dims):
    nx, nz, nc = dims
    along_z = [
        [(x * nz + z) * nc + c for z in range(nz)] for x in range(nx) for c in range(nc)
    ]
    in_plane = [
        [(x * nz + z) * nc + c for x in range(nx) for c in range(nc)] for z in range(nz)
    ]
    by_core = [
        [(x * nz + z) * nc + c for x in range(nx) for c in range(nc) for z in range(nz)]
    ]
    return along_z, in_plane, by_core


def picked_kernel(choose_ref, line_ref, *out_refs):
    rows = choose_ref.shape[1] // len(out_refs)
    for part in range(choose_ref.shape[0]):
        chosen = jnp.dot(
            choose_ref[part], line_ref[part], preferred_element_type=jnp.float32
        ).astype(jnp.bfloat16)
        for place, out_ref in enumerate(out_refs):
            out_ref[part * rows : (part + 1) * rows, :] = chosen[
                place * rows : (place + 1) * rows
            ]


def picked_rows(choose, line, places):
    parts, picks, depth = choose.shape
    width, tile = line.shape[2], 512
    out_rows = parts * picks // places
    return pl.pallas_call(
        picked_kernel,
        grid=(width // tile,),
        in_specs=[
            pl.BlockSpec((parts, picks, depth), lambda j: (0, 0, 0)),
            pl.BlockSpec((parts, depth, tile), lambda j: (0, 0, j)),
        ],
        out_specs=[pl.BlockSpec((out_rows, tile), lambda j: (0, j))] * places,
        out_shape=[jax.ShapeDtypeStruct((out_rows, width), jnp.bfloat16)] * places,
        compiler_params=pltpu.CompilerParams(vmem_limit_bytes=40 * 2**20),
        cost_estimate=pl.CostEstimate(
            flops=2 * parts * picks * depth * width,
            bytes_accessed=2 * (choose.size + line.size + parts * picks * width),
            transcendentals=0,
        ),
    )(choose, line)


def outer_kernel(*refs):
    *cot_refs, hid_ref, out_ref = refs
    out_ref[...] = lax.dot_general(
        jnp.concatenate([ref[...] for ref in cot_refs]),
        hid_ref[...],
        (((0,), (0,)), ((), ())),
        preferred_element_type=jnp.float32,
    ).astype(jnp.bfloat16)


def outer_sum(cot_parts, hid_rows):
    rows, hidden = hid_rows.shape
    width, tile = cot_parts[0].shape[1], 512
    return pl.pallas_call(
        outer_kernel,
        grid=(width // tile,),
        in_specs=[pl.BlockSpec((part.shape[0], tile), lambda j: (0, j)) for part in cot_parts]
        + [pl.BlockSpec((rows, hidden), lambda j: (0, 0))],
        out_specs=pl.BlockSpec((tile, hidden), lambda j: (j, 0)),
        out_shape=jax.ShapeDtypeStruct((width, hidden), jnp.bfloat16),
        compiler_params=pltpu.CompilerParams(vmem_limit_bytes=40 * 2**20),
        cost_estimate=pl.CostEstimate(
            flops=2 * rows * width * hidden,
            bytes_accessed=2 * (rows * (width + hidden) + width * hidden),
            transcendentals=0,
        ),
    )(*cot_parts, hid_rows)


def on_device(dims, down_cotangent, saved_hidden, route_ids, route_gates, down_weight):
    nx, nz, nc = dims
    along_z, in_plane, by_core = grid_of(dims)
    experts, plane = nx * nz * nc, nx * nc
    tokens, top = route_ids.shape
    width, hidden = down_cotangent.shape[1], saved_hidden.shape[2]
    pairs, rows = tokens * top, experts * SLOTS
    lanes = SLOTS * hidden // 128

    ids = route_ids.T
    gates = route_gates.T.reshape(pairs, 1).astype(jnp.float32)
    hid = saved_hidden.transpose(1, 0, 2).reshape(pairs, hidden).astype(jnp.float32)

    named = ids[:, None, :] == jnp.arange(experts, dtype=jnp.int32)[None, :, None]
    member = jnp.any(named, axis=0)
    earlier = jnp.arange(tokens)[:, None] < jnp.arange(tokens)[None, :]
    rank = jnp.dot(
        member.astype(jnp.bfloat16),
        earlier.astype(jnp.bfloat16),
        preferred_element_type=jnp.float32,
    ).astype(jnp.int32)
    within = jnp.sum(jnp.where(named, rank[None], 0), axis=1)

    slot = jnp.arange(SLOTS, dtype=jnp.int32)
    table = jnp.max(
        jnp.where(
            member[:, None, :] & (rank[:, None, :] == slot[None, :, None]),
            jnp.arange(tokens, dtype=jnp.int32)[None, None, :],
            -1,
        ),
        axis=2,
    )
    table = table.reshape(nx, nz, nc * SLOTS).transpose(1, 0, 2).reshape(nz, 1, plane * SLOTS)
    place = lax.axis_index("expert")
    my_x, my_z, my_c = place // (nz * nc), place // nc % nz, place % nc

    def permuted(source, block):
        pattern = source[:, None] == jnp.arange(block.shape[0], dtype=jnp.int32)[None, :]
        return jnp.dot(
            pattern.astype(jnp.bfloat16), block, preferred_element_type=jnp.float32
        ).astype(jnp.bfloat16)

    def swapped(block, groups):
        return lax.all_to_all(
            block, "expert", 0, 0, axis_index_groups=groups, tiled=True
        )

    replicas, replica = lax.axis_size("dp"), lax.axis_index("dp")
    own = down_weight[0]
    weight = jnp.zeros((replicas,) + own.shape, own.dtype)
    for step in range(replicas):
        block = own
        if step:
            block = lax.ppermute(
                own, "dp", [(i, (i - step) % replicas) for i in range(replicas)]
            )
        weight = lax.dynamic_update_index_in_dim(
            weight, block, (replica + step) % replicas, 0
        )
    weight = weight.reshape(width, hidden)

    scaled = (gates * hid).astype(jnp.bfloat16)
    ex, ez, ec = ids // (nz * nc), ids // nc % nz, ids % nc
    by_plane = (((ex * nc + ec) * nz + ez) * SLOTS + within).reshape(pairs)
    send = jnp.arange(rows, dtype=jnp.int32)[:, None] == by_plane[None, :]
    sent = jnp.dot(send.astype(jnp.bfloat16), scaled, preferred_element_type=jnp.float32)
    sent = swapped(sent.astype(jnp.bfloat16).reshape(plane, nz * SLOTS, hidden), in_plane)
    sent, table = lax.optimization_barrier((sent, table))
    table = swapped(table, along_z).reshape(nz, plane, SLOTS)
    order = np.arange(rows).reshape(plane, nz, SLOTS).transpose(1, 0, 2).reshape(rows)
    sent = permuted(jnp.asarray(order, jnp.int32), sent.reshape(rows, hidden))
    sent = sent.reshape(nz, plane * SLOTS, hidden)

    line = lax.all_gather(
        down_cotangent, "expert", axis_index_groups=along_z, axis=0, tiled=True
    )
    line, sent, table, weight = lax.optimization_barrier((line, sent, table, weight))

    work_hid = swapped(sent, along_z).reshape(rows, hidden)
    half = nz // 2
    line = line.reshape(2, half * tokens, width)
    offset = (jnp.arange(nz, dtype=jnp.int32) % half * tokens)[:, None, None]
    pick = jnp.where(table >= 0, table + offset, -1)
    pick = pick.reshape(2, half, nx, nc, SLOTS).transpose(2, 3, 0, 1, 4)
    pick = jnp.roll(jnp.roll(pick, -my_x, axis=0), -my_c, axis=1)
    pick = pick.reshape(plane, 2, half * SLOTS).transpose(1, 0, 2)
    pick = pick.reshape(2, plane * half * SLOTS, 1)
    token = jnp.arange(half * tokens, dtype=jnp.int32)
    choose = (pick == token).astype(jnp.bfloat16)
    chosen = picked_rows(choose, line, plane)

    work_cot = []
    back = jnp.zeros((plane, nz * SLOTS, hidden), jnp.bfloat16)
    for dx, dc in ((0, 0), (0, 1), (1, 0), (1, 1), (3, 0), (3, 1), (2, 0), (2, 1)):
        part = chosen[dx * nc + dc]
        if dx or dc:
            moves = [
                ((x * nz + z) * nc + c, ((x + dx) % nx * nz + z) * nc + (c + dc) % nc)
                for x in range(nx)
                for z in range(nz)
                for c in range(nc)
            ]
            part = lax.ppermute(part, "expert", moves)
        work_cot.append(part)
        grad_rows = jnp.dot(part, weight, preferred_element_type=jnp.float32)
        source = (my_x - dx) % nx * nc + (my_c - dc) % nc
        back = lax.dynamic_update_index_in_dim(back, grad_rows.astype(jnp.bfloat16), source, 0)
    home = swapped(back.reshape(experts, lanes, 128), by_core).reshape(rows, hidden)

    held = []
    for dx, dc in ((0, 0), (0, 1), (1, 0), (1, 1), (3, 0), (3, 1), (2, 0), (2, 1)):
        source = (my_x - dx) % nx * nc + (my_c - dc) % nc
        at = jnp.arange(nz * SLOTS, dtype=jnp.int32)
        held.append((at // SLOTS * plane + source) * SLOTS + at % SLOTS)
    total = outer_sum(work_cot, permuted(jnp.concatenate(held), work_hid))
    weight_grad = lax.psum_scatter(total, "dp", scatter_dimension=0, tiled=True)

    take = (by_plane[:, None] == jnp.arange(rows, dtype=jnp.int32)[None, :]).astype(jnp.bfloat16)
    mine = jnp.dot(take, home, preferred_element_type=jnp.float32)
    hidden_grad = (gates * mine).astype(jnp.bfloat16)
    gate_grad = jnp.sum(mine * hid, axis=1).astype(jnp.bfloat16)
    hidden_grad = hidden_grad.reshape(top, tokens, hidden).transpose(1, 0, 2)
    return hidden_grad, gate_grad.reshape(top, tokens).T, weight_grad[None]


def solution(mesh):
    dims = (4, 16, 2)
    in_specs = (
        P(("dp", "expert"), None),
        P(("dp", "expert"), None, None),
        P(("dp", "expert"), None),
        P(("dp", "expert"), None),
        P("expert", "dp", None),
    )
    out_specs = (
        P(("dp", "expert"), None, None),
        P(("dp", "expert"), None),
        P("expert", "dp", None),
    )

    def step(*arrays):
        return on_device(dims, *arrays)

    return jax.shard_map(
        step, mesh=mesh, in_specs=in_specs, out_specs=out_specs, check_vma=False
    )
```

```python
import jax
import jax.numpy as jnp
import numpy as np
from jax import lax
from jax.experimental import pallas as pl
from jax.experimental.pallas import tpu as pltpu
from jax.sharding import PartitionSpec as P

SLOTS = 10
GROUP = 4
VMEM = 60 * 2**20
PLACES = ((0, 0), (2, 0), (1, 0), (3, 0), (2, 1), (1, 1), (3, 1), (0, 1))
DONE_ORDER = (0, 1, 2, 3, 4, 7, 6, 5)


def grid_of(dims):
    nx, nz, nc = dims
    along_z = [
        [(x * nz + z) * nc + c for z in range(nz)] for x in range(nx) for c in range(nc)
    ]
    in_plane = [
        [(x * nz + z) * nc + c for x in range(nx) for c in range(nc)] for z in range(nz)
    ]
    by_core = [
        [(x * nz + z) * nc + c for x in range(nx) for c in range(nc) for z in range(nz)]
    ]
    return along_z, in_plane, by_core


def picked_kernel(choose_ref, line_ref, *out_refs):
    lower, upper = [
        jnp.dot(choose_ref[part], line_ref[part], preferred_element_type=jnp.float32)
        for part in range(2)
    ]
    rows = lower.shape[0] // len(out_refs)
    for place, out_ref in enumerate(out_refs):
        chosen = slice(place * rows, (place + 1) * rows)
        out_ref[...] = jnp.concatenate([lower[chosen], upper[chosen]]).astype(jnp.bfloat16)


def picked_rows(choose, line, places):
    parts, picks, depth = choose.shape
    width, tile = line.shape[2], line.shape[2] // 2
    out_rows = parts * picks // places
    return pl.pallas_call(
        picked_kernel,
        grid=(parts // 2, width // tile),
        in_specs=[
            pl.BlockSpec((2, picks, depth), lambda i, j: (i, 0, 0)),
            pl.BlockSpec((2, depth, tile), lambda i, j: (i, 0, j)),
        ],
        out_specs=[pl.BlockSpec((2 * picks // places, tile), lambda i, j: (i, j))] * places,
        out_shape=[jax.ShapeDtypeStruct((out_rows, width), jnp.bfloat16)] * places,
        compiler_params=pltpu.CompilerParams(vmem_limit_bytes=VMEM),
        cost_estimate=pl.CostEstimate(
            flops=2 * parts * picks * depth * width,
            bytes_accessed=2 * (choose.size + line.size + parts * picks * width),
            transcendentals=0,
        ),
    )(choose, line)


def outer_kernel(*refs):
    *cot_refs, hid_ref, out_ref = refs
    out_ref[...] = lax.dot_general(
        jnp.concatenate([ref[...] for ref in cot_refs]),
        hid_ref[...],
        (((0,), (0,)), ((), ())),
        preferred_element_type=jnp.float32,
    ).astype(jnp.bfloat16)


def outer_sum(cot_parts, hid_rows):
    rows, hidden = hid_rows.shape
    width, tile = cot_parts[0].shape[1], 256
    return pl.pallas_call(
        outer_kernel,
        grid=(width // tile,),
        in_specs=[pl.BlockSpec((part.shape[0], tile), lambda j: (0, j)) for part in cot_parts]
        + [pl.BlockSpec((rows, hidden), lambda j: (0, 0))],
        out_specs=pl.BlockSpec((tile, hidden), lambda j: (j, 0)),
        out_shape=jax.ShapeDtypeStruct((width, hidden), jnp.bfloat16),
        compiler_params=pltpu.CompilerParams(vmem_limit_bytes=VMEM),
        cost_estimate=pl.CostEstimate(
            flops=2 * rows * width * hidden,
            bytes_accessed=2 * (rows * (width + hidden) + width * hidden),
            transcendentals=0,
        ),
    )(*cot_parts, hid_rows)


def on_device(dims, down_cotangent, saved_hidden, route_ids, route_gates, down_weight):
    nx, nz, nc = dims
    along_z, in_plane, by_core = grid_of(dims)
    experts, plane = nx * nz * nc, nx * nc
    tokens, top = route_ids.shape
    width, hidden = down_cotangent.shape[1], saved_hidden.shape[2]
    pairs, rows = tokens * top, experts * SLOTS
    lanes = SLOTS * hidden // 128

    ids = route_ids.T
    gates = route_gates.T.reshape(pairs, 1).astype(jnp.float32)
    hid = saved_hidden.transpose(1, 0, 2).reshape(pairs, hidden).astype(jnp.float32)

    named = ids[:, None, :] == jnp.arange(experts, dtype=jnp.int32)[None, :, None]
    member = jnp.any(named, axis=0)
    earlier = jnp.arange(tokens)[:, None] < jnp.arange(tokens)[None, :]
    rank = jnp.dot(
        member.astype(jnp.bfloat16),
        earlier.astype(jnp.bfloat16),
        preferred_element_type=jnp.float32,
    ).astype(jnp.int32)
    within = jnp.sum(jnp.where(named, rank[None], 0), axis=1)

    slot = jnp.arange(SLOTS, dtype=jnp.int32)
    table = jnp.max(
        jnp.where(
            member[:, None, :] & (rank[:, None, :] == slot[None, :, None]),
            jnp.arange(tokens, dtype=jnp.int32)[None, None, :],
            -1,
        ),
        axis=2,
    )
    table = table.reshape(nx, nz, nc * SLOTS).transpose(1, 0, 2).reshape(nz, 1, plane * SLOTS)
    place = lax.axis_index("expert")
    my_x, my_z, my_c = place // (nz * nc), place // nc % nz, place % nc

    def permuted(source, block):
        pattern = source[:, None] == jnp.arange(block.shape[0], dtype=jnp.int32)[None, :]
        return jnp.dot(
            pattern.astype(jnp.bfloat16), block, preferred_element_type=jnp.float32
        ).astype(jnp.bfloat16)

    def swapped(block, groups):
        return lax.all_to_all(
            block, "expert", 0, 0, axis_index_groups=groups, tiled=True
        )

    replicas, replica = lax.axis_size("dp"), lax.axis_index("dp")
    own = down_weight[0]
    weight = jnp.zeros((replicas,) + own.shape, own.dtype)
    for step in range(replicas):
        block = own
        if step:
            block = lax.ppermute(
                own, "dp", [(i, (i - step) % replicas) for i in range(replicas)]
            )
        weight = lax.dynamic_update_index_in_dim(
            weight, block, (replica + step) % replicas, 0
        )
    weight = weight.reshape(width, hidden)

    scaled = (gates * hid).astype(jnp.bfloat16)
    ex, ez, ec = ids // (nz * nc), ids // nc % nz, ids % nc
    by_plane = (((ex * nc + ec) * nz + ez) * SLOTS + within).reshape(pairs)
    send = jnp.arange(rows, dtype=jnp.int32)[:, None] == by_plane[None, :]
    sent = jnp.dot(send.astype(jnp.bfloat16), scaled, preferred_element_type=jnp.float32)
    sent = swapped(sent.astype(jnp.bfloat16).reshape(plane, nz * SLOTS, hidden), in_plane)
    sent, table = lax.optimization_barrier((sent, table))
    table = swapped(table, along_z).reshape(nz, plane, SLOTS)
    order = np.arange(rows).reshape(plane, nz, SLOTS).transpose(1, 0, 2).reshape(rows)
    sent = permuted(jnp.asarray(order, jnp.int32), sent.reshape(rows, hidden))
    sent = sent.reshape(nz, plane * SLOTS, hidden)

    line = lax.all_gather(
        down_cotangent, "expert", axis_index_groups=along_z, axis=0, tiled=True
    )
    pick = jnp.where(
        table >= 0, table + (jnp.arange(nz) % GROUP * tokens)[:, None, None], -1
    )
    pick = pick.reshape(nz, nx, nc, SLOTS).transpose(1, 2, 0, 3)
    pick = jnp.roll(jnp.roll(pick, -my_x, axis=0), -my_c, axis=1)
    pick = pick.reshape(plane, nz // GROUP, GROUP * SLOTS).transpose(1, 0, 2)
    pick = pick.reshape(nz // GROUP, plane * GROUP * SLOTS, 1)
    choose = (pick == jnp.arange(GROUP * tokens, dtype=jnp.int32)).astype(jnp.bfloat16)
    line, sent, choose, weight = lax.optimization_barrier((line, sent, choose, weight))

    work_hid = swapped(sent, along_z).reshape(rows, hidden)
    chosen = picked_rows(choose, line.reshape(nz // GROUP, GROUP * tokens, width), plane)

    work_cot = []
    for dx, dc in PLACES:
        part = chosen[dx * nc + dc]
        if dx or dc:
            moves = [
                ((x * nz + z) * nc + c, ((x + dx) % nx * nz + z) * nc + (c + dc) % nc)
                for x in range(nx)
                for z in range(nz)
                for c in range(nc)
            ]
            part = lax.ppermute(part, "expert", moves)
        work_cot.append(part)
    sources = [(my_x - dx) % nx * nc + (my_c - dc) % nc for dx, dc in PLACES]
    back = jnp.zeros((plane, nz * SLOTS, hidden), jnp.bfloat16)
    for part in DONE_ORDER:
        grads = jnp.dot(work_cot[part], weight, preferred_element_type=jnp.float32)
        back = lax.dynamic_update_index_in_dim(
            back, grads.astype(jnp.bfloat16), sources[part], 0
        )
    home = swapped(back.reshape(experts, lanes, 128), by_core).reshape(rows, hidden)

    held = []
    for source in sources:
        at = jnp.arange(nz * SLOTS, dtype=jnp.int32)
        held.append((at // SLOTS * plane + source) * SLOTS + at % SLOTS)
    total = outer_sum(work_cot, permuted(jnp.concatenate(held), work_hid))
    weight_grad = lax.psum_scatter(total, "dp", scatter_dimension=0, tiled=True)

    take = (by_plane[:, None] == jnp.arange(rows, dtype=jnp.int32)[None, :]).astype(jnp.bfloat16)
    mine = jnp.dot(take, home, preferred_element_type=jnp.float32)
    hidden_grad = (gates * mine).astype(jnp.bfloat16)
    gate_grad = jnp.sum(mine * hid, axis=1).astype(jnp.bfloat16)
    hidden_grad = hidden_grad.reshape(top, tokens, hidden).transpose(1, 0, 2)
    return hidden_grad, gate_grad.reshape(top, tokens).T, weight_grad[None]


def solution(mesh):
    dims = (4, 16, 2)
    in_specs = (
        P(("dp", "expert"), None),
        P(("dp", "expert"), None, None),
        P(("dp", "expert"), None),
        P(("dp", "expert"), None),
        P("expert", "dp", None),
    )
    out_specs = (
        P(("dp", "expert"), None, None),
        P(("dp", "expert"), None),
        P("expert", "dp", None),
    )

    def step(*arrays):
        return on_device(dims, *arrays)

    return jax.shard_map(
        step, mesh=mesh, in_specs=in_specs, out_specs=out_specs, check_vma=False
    )
```

```python
import jax
import jax.numpy as jnp
import numpy as np
from jax import lax
from jax.experimental import pallas as pl
from jax.experimental.pallas import tpu as pltpu
from jax.sharding import PartitionSpec as P

SLOTS = 10
GROUP = 4
VMEM = 60 * 2**20
PLACES = ((0, 0), (2, 0), (1, 0), (3, 0), (2, 1), (1, 1), (3, 1), (0, 1))
DONE_ORDER = (0, 1, 2, 3, 4, 7, 5, 6)


def grid_of(dims):
    nx, nz, nc = dims
    along_z = [
        [(x * nz + z) * nc + c for z in range(nz)] for x in range(nx) for c in range(nc)
    ]
    in_plane = [
        [(x * nz + z) * nc + c for x in range(nx) for c in range(nc)] for z in range(nz)
    ]
    by_core = [
        [(x * nz + z) * nc + c for x in range(nx) for c in range(nc) for z in range(nz)]
    ]
    return along_z, in_plane, by_core


def picked_kernel(choose_ref, line_ref, *out_refs):
    lower, upper = [
        jnp.dot(choose_ref[part], line_ref[part], preferred_element_type=jnp.float32)
        for part in range(2)
    ]
    rows = lower.shape[0] // len(out_refs)
    for place, out_ref in enumerate(out_refs):
        chosen = slice(place * rows, (place + 1) * rows)
        out_ref[...] = jnp.concatenate([lower[chosen], upper[chosen]]).astype(jnp.bfloat16)


def picked_rows(choose, line, places):
    parts, picks, depth = choose.shape
    width, tile = line.shape[2], line.shape[2] // 2
    out_rows = parts * picks // places
    return pl.pallas_call(
        picked_kernel,
        grid=(parts // 2, width // tile),
        in_specs=[
            pl.BlockSpec((2, picks, depth), lambda i, j: (i, 0, 0)),
            pl.BlockSpec((2, depth, tile), lambda i, j: (i, 0, j)),
        ],
        out_specs=[pl.BlockSpec((2 * picks // places, tile), lambda i, j: (i, j))] * places,
        out_shape=[jax.ShapeDtypeStruct((out_rows, width), jnp.bfloat16)] * places,
        compiler_params=pltpu.CompilerParams(vmem_limit_bytes=VMEM),
        cost_estimate=pl.CostEstimate(
            flops=2 * parts * picks * depth * width,
            bytes_accessed=2 * (choose.size + line.size + parts * picks * width),
            transcendentals=0,
        ),
    )(choose, line)


def outer_kernel(*refs):
    *cot_refs, hid_ref, out_ref = refs
    out_ref[...] = lax.dot_general(
        jnp.concatenate([ref[...] for ref in cot_refs]),
        hid_ref[...],
        (((0,), (0,)), ((), ())),
        preferred_element_type=jnp.float32,
    ).astype(jnp.bfloat16)


def outer_sum(cot_parts, hid_rows):
    rows, hidden = hid_rows.shape
    width, tile = cot_parts[0].shape[1], 256
    return pl.pallas_call(
        outer_kernel,
        grid=(width // tile,),
        in_specs=[pl.BlockSpec((part.shape[0], tile), lambda j: (0, j)) for part in cot_parts]
        + [pl.BlockSpec((rows, hidden), lambda j: (0, 0))],
        out_specs=pl.BlockSpec((tile, hidden), lambda j: (j, 0)),
        out_shape=jax.ShapeDtypeStruct((width, hidden), jnp.bfloat16),
        compiler_params=pltpu.CompilerParams(vmem_limit_bytes=VMEM),
        cost_estimate=pl.CostEstimate(
            flops=2 * rows * width * hidden,
            bytes_accessed=2 * (rows * (width + hidden) + width * hidden),
            transcendentals=0,
        ),
    )(*cot_parts, hid_rows)


def on_device(dims, down_cotangent, saved_hidden, route_ids, route_gates, down_weight):
    nx, nz, nc = dims
    along_z, in_plane, by_core = grid_of(dims)
    experts, plane = nx * nz * nc, nx * nc
    tokens, top = route_ids.shape
    width, hidden = down_cotangent.shape[1], saved_hidden.shape[2]
    pairs, rows = tokens * top, experts * SLOTS
    lanes = SLOTS * hidden // 128

    ids = route_ids.T
    gates = route_gates.T.reshape(pairs, 1).astype(jnp.float32)
    hid = saved_hidden.transpose(1, 0, 2).reshape(pairs, hidden).astype(jnp.float32)

    named = ids[:, None, :] == jnp.arange(experts, dtype=jnp.int32)[None, :, None]
    member = jnp.any(named, axis=0)
    earlier = jnp.arange(tokens)[:, None] < jnp.arange(tokens)[None, :]
    rank = jnp.dot(
        member.astype(jnp.bfloat16),
        earlier.astype(jnp.bfloat16),
        preferred_element_type=jnp.float32,
    ).astype(jnp.int32)
    within = jnp.sum(jnp.where(named, rank[None], 0), axis=1)

    slot = jnp.arange(SLOTS, dtype=jnp.int32)
    table = jnp.max(
        jnp.where(
            member[:, None, :] & (rank[:, None, :] == slot[None, :, None]),
            jnp.arange(tokens, dtype=jnp.int32)[None, None, :],
            -1,
        ),
        axis=2,
    )
    table = table.reshape(nx, nz, nc * SLOTS).transpose(1, 0, 2).reshape(nz, 1, plane * SLOTS)
    place = lax.axis_index("expert")
    my_x, my_z, my_c = place // (nz * nc), place // nc % nz, place % nc

    def permuted(source, block):
        pattern = source[:, None] == jnp.arange(block.shape[0], dtype=jnp.int32)[None, :]
        return jnp.dot(
            pattern.astype(jnp.bfloat16), block, preferred_element_type=jnp.float32
        ).astype(jnp.bfloat16)

    def swapped(block, groups):
        return lax.all_to_all(
            block, "expert", 0, 0, axis_index_groups=groups, tiled=True
        )

    replicas, replica = lax.axis_size("dp"), lax.axis_index("dp")
    own = down_weight[0]
    weight = jnp.zeros((replicas,) + own.shape, own.dtype)
    for step in range(replicas):
        block = own
        if step:
            block = lax.ppermute(
                own, "dp", [(i, (i - step) % replicas) for i in range(replicas)]
            )
        weight = lax.dynamic_update_index_in_dim(
            weight, block, (replica + step) % replicas, 0
        )
    weight = weight.reshape(width, hidden)

    scaled = (gates * hid).astype(jnp.bfloat16)
    ex, ez, ec = ids // (nz * nc), ids // nc % nz, ids % nc
    by_plane = (((ex * nc + ec) * nz + ez) * SLOTS + within).reshape(pairs)
    send = jnp.arange(rows, dtype=jnp.int32)[:, None] == by_plane[None, :]
    sent = jnp.dot(send.astype(jnp.bfloat16), scaled, preferred_element_type=jnp.float32)
    sent = swapped(sent.astype(jnp.bfloat16).reshape(plane, nz * SLOTS, hidden), in_plane)
    sent, table = lax.optimization_barrier((sent, table))
    table = swapped(table, along_z).reshape(nz, plane, SLOTS)
    order = np.arange(rows).reshape(plane, nz, SLOTS).transpose(1, 0, 2).reshape(rows)
    sent = permuted(jnp.asarray(order, jnp.int32), sent.reshape(rows, hidden))
    sent = sent.reshape(nz, plane * SLOTS, hidden)

    line = lax.all_gather(
        down_cotangent, "expert", axis_index_groups=along_z, axis=0, tiled=True
    )
    pick = jnp.where(
        table >= 0, table + (jnp.arange(nz) % GROUP * tokens)[:, None, None], -1
    )
    pick = pick.reshape(nz, nx, nc, SLOTS).transpose(1, 2, 0, 3)
    pick = jnp.roll(jnp.roll(pick, -my_x, axis=0), -my_c, axis=1)
    pick = pick.reshape(plane, nz // GROUP, GROUP * SLOTS).transpose(1, 0, 2)
    pick = pick.reshape(nz // GROUP, plane * GROUP * SLOTS, 1)
    choose = (pick == jnp.arange(GROUP * tokens, dtype=jnp.int32)).astype(jnp.bfloat16)
    line, sent, choose, weight = lax.optimization_barrier((line, sent, choose, weight))

    work_hid = swapped(sent, along_z).reshape(rows, hidden)
    chosen = picked_rows(choose, line.reshape(nz // GROUP, GROUP * tokens, width), plane)

    work_cot = []
    for dx, dc in PLACES:
        part = chosen[dx * nc + dc]
        if dx or dc:
            moves = [
                ((x * nz + z) * nc + c, ((x + dx) % nx * nz + z) * nc + (c + dc) % nc)
                for x in range(nx)
                for z in range(nz)
                for c in range(nc)
            ]
            part = lax.ppermute(part, "expert", moves)
        work_cot.append(part)
    sources = [(my_x - dx) % nx * nc + (my_c - dc) % nc for dx, dc in PLACES]
    back = jnp.zeros((plane, nz * SLOTS, hidden), jnp.bfloat16)
    for part in DONE_ORDER:
        grads = jnp.dot(work_cot[part], weight, preferred_element_type=jnp.float32)
        back = lax.dynamic_update_index_in_dim(
            back, grads.astype(jnp.bfloat16), sources[part], 0
        )
    take = (by_plane[:, None] == jnp.arange(rows, dtype=jnp.int32)[None, :]).astype(jnp.bfloat16)
    take, back = lax.optimization_barrier((take, back))
    home = swapped(back.reshape(experts, lanes // 4, 4, 128), by_core).reshape(rows, hidden)

    held = []
    for source in sources:
        at = jnp.arange(nz * SLOTS, dtype=jnp.int32)
        held.append((at // SLOTS * plane + source) * SLOTS + at % SLOTS)
    total = outer_sum(work_cot, permuted(jnp.concatenate(held), work_hid))
    weight_grad = lax.psum_scatter(total, "dp", scatter_dimension=0, tiled=True)

    mine = jnp.dot(take, home, preferred_element_type=jnp.float32)
    hidden_grad = (gates * mine).astype(jnp.bfloat16)
    gate_grad = jnp.sum(mine * hid, axis=1).astype(jnp.bfloat16)
    hidden_grad = hidden_grad.reshape(top, tokens, hidden).transpose(1, 0, 2)
    return hidden_grad, gate_grad.reshape(top, tokens).T, weight_grad[None]


def solution(mesh):
    dims = (4, 16, 2)
    in_specs = (
        P(("dp", "expert"), None),
        P(("dp", "expert"), None, None),
        P(("dp", "expert"), None),
        P(("dp", "expert"), None),
        P("expert", "dp", None),
    )
    out_specs = (
        P(("dp", "expert"), None, None),
        P(("dp", "expert"), None),
        P("expert", "dp", None),
    )

    def step(*arrays):
        return on_device(dims, *arrays)

    return jax.shard_map(
        step, mesh=mesh, in_specs=in_specs, out_specs=out_specs, check_vma=False
    )
```

```python
import jax
import jax.numpy as jnp
import numpy as np
from jax import lax
from jax.experimental import pallas as pl
from jax.experimental.pallas import tpu as pltpu
from jax.sharding import PartitionSpec as P

SLOTS = 10
GROUP = 4
VMEM = 60 * 2**20
PLACES = ((0, 0), (2, 0), (1, 0), (3, 0), (2, 1), (1, 1), (3, 1), (0, 1))
DONE_ORDER = ((0,), (1,), (2,), (3,), (4,), (7,), (5, 6))


def grid_of(dims):
    nx, nz, nc = dims
    along_z = [
        [(x * nz + z) * nc + c for z in range(nz)] for x in range(nx) for c in range(nc)
    ]
    in_plane = [
        [(x * nz + z) * nc + c for x in range(nx) for c in range(nc)] for z in range(nz)
    ]
    by_core = [
        [(x * nz + z) * nc + c for x in range(nx) for c in range(nc) for z in range(nz)]
    ]
    return along_z, in_plane, by_core


def picked_kernel(choose_ref, line_ref, *out_refs):
    lower, upper = [
        jnp.dot(choose_ref[part], line_ref[part], preferred_element_type=jnp.float32)
        for part in range(2)
    ]
    rows = lower.shape[0] // len(out_refs)
    for place, out_ref in enumerate(out_refs):
        chosen = slice(place * rows, (place + 1) * rows)
        out_ref[...] = jnp.concatenate([lower[chosen], upper[chosen]]).astype(jnp.bfloat16)


def picked_rows(choose, line, places):
    parts, picks, depth = choose.shape
    width, tile = line.shape[2], line.shape[2] // 2
    out_rows = parts * picks // places
    return pl.pallas_call(
        picked_kernel,
        grid=(parts // 2, width // tile),
        in_specs=[
            pl.BlockSpec((2, picks, depth), lambda i, j: (i, 0, 0)),
            pl.BlockSpec((2, depth, tile), lambda i, j: (i, 0, j)),
        ],
        out_specs=[pl.BlockSpec((2 * picks // places, tile), lambda i, j: (i, j))] * places,
        out_shape=[jax.ShapeDtypeStruct((out_rows, width), jnp.bfloat16)] * places,
        compiler_params=pltpu.CompilerParams(vmem_limit_bytes=VMEM),
        cost_estimate=pl.CostEstimate(
            flops=2 * parts * picks * depth * width,
            bytes_accessed=2 * (choose.size + line.size + parts * picks * width),
            transcendentals=0,
        ),
    )(choose, line)


def outer_kernel(*refs):
    *cot_refs, hid_ref, out_ref = refs
    out_ref[...] = lax.dot_general(
        jnp.concatenate([ref[...] for ref in cot_refs]),
        hid_ref[...],
        (((0,), (0,)), ((), ())),
        preferred_element_type=jnp.float32,
    ).astype(jnp.bfloat16)


def outer_sum(cot_parts, hid_rows):
    rows, hidden = hid_rows.shape
    width, tile = cot_parts[0].shape[1], 256
    return pl.pallas_call(
        outer_kernel,
        grid=(width // tile,),
        in_specs=[pl.BlockSpec((part.shape[0], tile), lambda j: (0, j)) for part in cot_parts]
        + [pl.BlockSpec((rows, hidden), lambda j: (0, 0))],
        out_specs=pl.BlockSpec((tile, hidden), lambda j: (j, 0)),
        out_shape=jax.ShapeDtypeStruct((width, hidden), jnp.bfloat16),
        compiler_params=pltpu.CompilerParams(vmem_limit_bytes=VMEM),
        cost_estimate=pl.CostEstimate(
            flops=2 * rows * width * hidden,
            bytes_accessed=2 * (rows * (width + hidden) + width * hidden),
            transcendentals=0,
        ),
    )(*cot_parts, hid_rows)


def on_device(dims, down_cotangent, saved_hidden, route_ids, route_gates, down_weight):
    nx, nz, nc = dims
    along_z, in_plane, by_core = grid_of(dims)
    experts, plane = nx * nz * nc, nx * nc
    tokens, top = route_ids.shape
    width, hidden = down_cotangent.shape[1], saved_hidden.shape[2]
    pairs, rows = tokens * top, experts * SLOTS
    lanes = SLOTS * hidden // 128

    ids = route_ids.T
    gates = route_gates.T.reshape(pairs, 1).astype(jnp.float32)
    hid = saved_hidden.transpose(1, 0, 2).reshape(pairs, hidden).astype(jnp.float32)

    named = ids[:, None, :] == jnp.arange(experts, dtype=jnp.int32)[None, :, None]
    member = jnp.any(named, axis=0)
    earlier = jnp.arange(tokens)[:, None] < jnp.arange(tokens)[None, :]
    rank = jnp.dot(
        member.astype(jnp.bfloat16),
        earlier.astype(jnp.bfloat16),
        preferred_element_type=jnp.float32,
    ).astype(jnp.int32)
    within = jnp.sum(jnp.where(named, rank[None], 0), axis=1)

    slot = jnp.arange(SLOTS, dtype=jnp.int32)
    table = jnp.max(
        jnp.where(
            member[:, None, :] & (rank[:, None, :] == slot[None, :, None]),
            jnp.arange(tokens, dtype=jnp.int32)[None, None, :],
            -1,
        ),
        axis=2,
    )
    table = table.reshape(nx, nz, nc * SLOTS).transpose(1, 0, 2).reshape(nz, 1, plane * SLOTS)
    place = lax.axis_index("expert")
    my_x, my_z, my_c = place // (nz * nc), place // nc % nz, place % nc

    def permuted(source, block):
        pattern = source[:, None] == jnp.arange(block.shape[0], dtype=jnp.int32)[None, :]
        return jnp.dot(
            pattern.astype(jnp.bfloat16), block, preferred_element_type=jnp.float32
        ).astype(jnp.bfloat16)

    def swapped(block, groups):
        return lax.all_to_all(
            block, "expert", 0, 0, axis_index_groups=groups, tiled=True
        )

    replicas, replica = lax.axis_size("dp"), lax.axis_index("dp")
    own = down_weight[0]
    weight = jnp.zeros((replicas,) + own.shape, own.dtype)
    for step in range(replicas):
        block = own
        if step:
            block = lax.ppermute(
                own, "dp", [(i, (i - step) % replicas) for i in range(replicas)]
            )
        weight = lax.dynamic_update_index_in_dim(
            weight, block, (replica + step) % replicas, 0
        )
    weight = weight.reshape(width, hidden)

    scaled = (gates * hid).astype(jnp.bfloat16)
    ex, ez, ec = ids // (nz * nc), ids // nc % nz, ids % nc
    by_plane = (((ex * nc + ec) * nz + ez) * SLOTS + within).reshape(pairs)
    send = jnp.arange(rows, dtype=jnp.int32)[:, None] == by_plane[None, :]
    sent = jnp.dot(send.astype(jnp.bfloat16), scaled, preferred_element_type=jnp.float32)
    sent = swapped(sent.astype(jnp.bfloat16).reshape(plane, nz * SLOTS, hidden), in_plane)
    sent, table = lax.optimization_barrier((sent, table))
    table = swapped(table, along_z).reshape(nz, plane, SLOTS)
    order = np.arange(rows).reshape(plane, nz, SLOTS).transpose(1, 0, 2).reshape(rows)
    sent = permuted(jnp.asarray(order, jnp.int32), sent.reshape(rows, hidden))
    sent = sent.reshape(nz, plane * SLOTS, hidden)

    line = lax.all_gather(
        down_cotangent, "expert", axis_index_groups=along_z, axis=0, tiled=True
    )
    pick = jnp.where(
        table >= 0, table + (jnp.arange(nz) % GROUP * tokens)[:, None, None], -1
    )
    pick = pick.reshape(nz, nx, nc, SLOTS).transpose(1, 2, 0, 3)
    pick = jnp.roll(jnp.roll(pick, -my_x, axis=0), -my_c, axis=1)
    pick = pick.reshape(plane, nz // GROUP, GROUP * SLOTS).transpose(1, 0, 2)
    pick = pick.reshape(nz // GROUP, plane * GROUP * SLOTS, 1)
    choose = (pick == jnp.arange(GROUP * tokens, dtype=jnp.int32)).astype(jnp.bfloat16)
    line, sent, choose, weight = lax.optimization_barrier((line, sent, choose, weight))

    work_hid = swapped(sent, along_z).reshape(rows, hidden)
    chosen = picked_rows(choose, line.reshape(nz // GROUP, GROUP * tokens, width), plane)

    work_cot = []
    for dx, dc in PLACES:
        part = chosen[dx * nc + dc]
        if dx or dc:
            moves = [
                ((x * nz + z) * nc + c, ((x + dx) % nx * nz + z) * nc + (c + dc) % nc)
                for x in range(nx)
                for z in range(nz)
                for c in range(nc)
            ]
            part = lax.ppermute(part, "expert", moves)
        work_cot.append(part)
    sources = [(my_x - dx) % nx * nc + (my_c - dc) % nc for dx, dc in PLACES]
    back = jnp.zeros((plane, nz * SLOTS, hidden), jnp.bfloat16)
    for parts in DONE_ORDER:
        joined = jnp.concatenate([work_cot[part] for part in parts])
        grads = jnp.dot(joined, weight, preferred_element_type=jnp.float32)
        grads = grads.astype(jnp.bfloat16).reshape(len(parts), nz * SLOTS, hidden)
        for at, part in enumerate(parts):
            back = lax.dynamic_update_index_in_dim(back, grads[at], sources[part], 0)
    take = (by_plane[:, None] == jnp.arange(rows, dtype=jnp.int32)[None, :]).astype(jnp.bfloat16)
    take, back = lax.optimization_barrier((take, back))
    home = swapped(back.reshape(experts, lanes // 4, 4, 128), by_core).reshape(rows, hidden)

    held = []
    for source in sources:
        at = jnp.arange(nz * SLOTS, dtype=jnp.int32)
        held.append((at // SLOTS * plane + source) * SLOTS + at % SLOTS)
    total = outer_sum(work_cot, permuted(jnp.concatenate(held), work_hid))
    weight_grad = lax.psum_scatter(total, "dp", scatter_dimension=0, tiled=True)

    mine = jnp.dot(take, home, preferred_element_type=jnp.float32)
    hidden_grad = (gates * mine).astype(jnp.bfloat16)
    gate_grad = jnp.sum(mine * hid, axis=1).astype(jnp.bfloat16)
    hidden_grad = hidden_grad.reshape(top, tokens, hidden).transpose(1, 0, 2)
    return hidden_grad, gate_grad.reshape(top, tokens).T, weight_grad[None]


def solution(mesh):
    dims = (4, 16, 2)
    in_specs = (
        P(("dp", "expert"), None),
        P(("dp", "expert"), None, None),
        P(("dp", "expert"), None),
        P(("dp", "expert"), None),
        P("expert", "dp", None),
    )
    out_specs = (
        P(("dp", "expert"), None, None),
        P(("dp", "expert"), None),
        P("expert", "dp", None),
    )

    def step(*arrays):
        return on_device(dims, *arrays)

    return jax.shard_map(
        step, mesh=mesh, in_specs=in_specs, out_specs=out_specs, check_vma=False
    )
```
